32 devices in a mesh: emit: 8 (over z, x), vx: 2 (over y), vy: 2 (over core).
Axes of the slice: x: 2, y: 2, z: 4, core: 2. Of those that a mesh axis runs over, the one named last changes fastest.
Arguments:
- fwd_state: float32 [3, 8, 512, 512], P(None, 'emit', 'vx', 'vy'), may hold values from -6 to 6
- adj_state: float32 [3, 8, 512, 512], P(None, 'emit', 'vx', 'vy'), may hold values from -6 to 6
- courant: float32 [512, 512], P('vx', 'vy'), may hold values from 0.2 to 0.45
- decay_rate: float32 [512, 512], P('vx', 'vy'), may hold values from 0.2 to 0.9
- strength: float32 [512, 512], P('vx', 'vy'), may hold values from 0.05 to 0.4
- footprint: int32 [8, 2, 2, 16], P('emit', 'vx', 'vy'), may hold values from 0 to 31, all different within a row
- owner_map: int32 [2, 2, 32], P('vx', 'vy'), may hold values from 0 to 31, each once within a row
Outputs:
- gradient: float32 [32, 32, 256], P('emit', 'vx', 'vy')
- pressure: float32 [8, 512, 512], P('emit', 'vx', 'vy')
The draws below stay inside these ranges and needn't reach their ends.
Inputs may be any that keep to these rules, and one draw needn't show every extreme that they name: `footprint`: in each row the 16 ids are distinct block ids of one tile. `owner_map`: for each tile a permutation of its 32 block ids.
All inputs are finite; a program needn't handle non-finite values.
Results may differ from the reference program's by a relative error of at most 0.0003.
Values sent between devices are 32-bit elements; how exact they have to be, the bound alone decides.
A program may use at most 64 MiB of HBM per device.

```python
import jax
import jax.numpy as jnp
from jax import lax

BR = 16
BC = 128
BX = 16
BY = 2
STEPS = 4
NB = 32
FP = 16
GROUPS = 8
NX = 512
NY = 512
N_VX = 2
N_VY = 2


def block_levels(own_key, extent, pieces, smallest, largest):
    gain = 1.0
    for axis_at, shards_of in pieces:
        steps = jax.random.uniform(jax.random.fold_in(jax.random.fold_in(own_key, 6), axis_at), (shards_of,), jnp.float32, smallest / len(pieces), largest / len(pieces))
        gain = gain * jnp.repeat(jnp.exp(steps), extent[axis_at] // shards_of).reshape((-1,) + (1,) * (len(extent) - 1 - axis_at))
    return gain


def different_ones(key, rows, amount, top, lift):
    order = jax.random.permutation(jax.random.fold_in(key, 1), amount)
    favour = order
    for power in range(3):
        favour = favour * favour // amount
    favour = favour * lift // amount
    chance = jax.random.randint(jax.random.fold_in(key, 2), (rows, amount), 0, 4096) + favour
    fixed_rows = jax.random.permutation(jax.random.fold_in(key, 3), rows)[jnp.arange(amount) % rows]
    chance = jnp.where(jnp.arange(rows)[:, None] == fixed_rows[None, :], 1 << 14, chance)
    score = chance * amount + jnp.arange(amount)
    return lax.top_k(score.astype(jnp.int32), top)[1].astype(jnp.int32)


def noise(rng, shape, width, reach, split=(), held_as=jnp.bfloat16):
    factor_of = block_levels(rng, shape, split, -0.22, 0.18) if split else 1.0
    values = jax.random.normal(rng, shape, jnp.float32) * width * factor_of
    return jnp.minimum(jnp.maximum(values, -reach), reach).astype(held_as)


def setup_inputs(seed: int = 0) -> dict:
    seeds = jax.random.split(jax.random.key(seed), 8)
    fwd_state = noise(seeds[0], (3, GROUPS, NX, NY), 1.0, 6.0, ((1, 8), (2, 2), (3, 2)), jnp.float32)
    adj_state = noise(seeds[1], (3, GROUPS, NX, NY), 1.0, 6.0, ((1, 8), (2, 2), (3, 2)), jnp.float32)
    courant = jnp.clip(0.2 + 0.24999999 * jax.random.uniform(seeds[2], (NX, NY), jnp.float32) ** block_levels(seeds[2], (NX, NY), ((0, 2), (1, 2)), -0.2, 0.2), 0.2, 0.45)
    decay_rate = jnp.clip(0.2 + 0.7 * jax.random.uniform(seeds[3], (NX, NY), jnp.float32) ** block_levels(seeds[3], (NX, NY), ((0, 2), (1, 2)), -0.2, 0.2), 0.2, 0.9)
    strength = jnp.clip(0.05 + 0.35 * jax.random.uniform(seeds[4], (NX, NY), jnp.float32) ** block_levels(seeds[4], (NX, NY), ((0, 2), (1, 2)), -0.2, 0.2), 0.05, 0.4)
    footprint = different_ones(seeds[5], GROUPS * N_VX * N_VY, NB, FP, 4096).reshape((GROUPS, N_VX, N_VY, FP))
    owner_map = jax.vmap(lambda own: jax.random.permutation(own, NB))(jax.random.split(seeds[6], N_VX * N_VY)).reshape((N_VX, N_VY, NB)).astype(jnp.int32)
    return dict(fwd_state=fwd_state, adj_state=adj_state, courant=courant, decay_rate=decay_rate, strength=strength, footprint=footprint, owner_map=owner_map)


def laplace(field):
    padded = jnp.pad(field, 1)
    return padded[2:, 1:-1] + padded[:-2, 1:-1] + padded[1:-1, 2:] + padded[1:-1, :-2] - 4.0 * field


def keep_all(field):
    return field


def advance(state, courant, decay_rate, strength, laplace_fn):
    former, current, memory = state
    curve = laplace_fn(current)
    memory = decay_rate * memory + strength * curve
    following = 2.0 * current - former + courant * (curve - memory)
    return (current, following, memory)


def propagate(state, courant, decay_rate, strength, laplace_fn, crop):
    levels = [crop(state[0]), crop(state[1])]
    for number in range(STEPS):
        state = advance(state, courant, decay_rate, strength, laplace_fn)
        levels.append(crop(state[1]))
    return levels


def imaging(forward, adjoint, scale):
    result = None
    for level in range(1, STEPS + 1):
        second = forward[level + 1] - 2.0 * forward[level] + forward[level - 1]
        term = adjoint[STEPS + 2 - level] * second
        result = term if result is None else result + term
    return result * scale


def reference(fwd_state, adj_state, courant, decay_rate, strength, footprint, owner_map):
    scale = 1.0 / GROUPS
    block_ids = jnp.arange(NB, dtype=jnp.int32)

    def per_group(total, inputs):
        forward_in, adjoint_in, listed = inputs
        forward = propagate((forward_in[0], forward_in[1], forward_in[2]), courant, decay_rate, strength, laplace, keep_all)
        adjoint = propagate((adjoint_in[0], adjoint_in[1], adjoint_in[2]), courant, decay_rate, strength, laplace, keep_all)
        gradient = imaging(forward, adjoint, scale)
        tiled = gradient.reshape(N_VX, BX, BR, N_VY, BY, BC).transpose(0, 3, 1, 4, 2, 5).reshape(N_VX, N_VY, NB, BR, BC)
        hits = jnp.any(listed[:, :, :, None] == block_ids, axis=2).astype(jnp.float32)
        return total + tiled * hits[:, :, :, None, None], forward[STEPS + 1]

    start = jnp.zeros((N_VX, N_VY, NB, BR, BC), jnp.float32)
    total, pressure = lax.scan(per_group, start, (jnp.moveaxis(fwd_state, 1, 0), jnp.moveaxis(adj_state, 1, 0), footprint))
    slots = jnp.take_along_axis(total, owner_map[:, :, :, None, None], axis=2)
    gradient_out = slots.transpose(2, 0, 3, 1, 4).reshape(NB, N_VX * BR, N_VY * BC)
    return gradient_out, pressure
```

```python
import functools

import jax
import jax.numpy as jnp
from jax import lax
from jax.experimental import pallas as pl
from jax.experimental.pallas import tpu as pltpu
from jax.sharding import PartitionSpec as P

BR = 16
BC = 128
STEPS = 4
TOP = 16
HALO = 8
CHUNK = 16
MESH = pl.DeviceIdType.MESH


def laplace_rows(state, field, row, count, cols, lane, east_on, west_on):
    center = [state[field, j, pl.ds(row, count), :] for j in range(3)]
    east = [pltpu.roll(center[j], BC - 1, 1) for j in range(3)]
    west = [pltpu.roll(center[j], 1, 1) for j in range(3)]
    curves = []
    for j in range(cols):
        after = east[(j + 1) % 3]
        before = west[(j + 2) % 3]
        if j == 1:
            after = after * east_on
        if j == 0:
            before = before * west_on
        right = jnp.where(lane == BC - 1, after, east[j])
        left = jnp.where(lane == 0, before, west[j])
        up = state[field, j, pl.ds(row - 1, count), :]
        down = state[field, j, pl.ds(row + 1, count), :]
        curves.append((up + down) + (left + right) - 4.0 * center[j])
    return center, curves


def kernel(n_emit, n_vx, rows, fwd, adj, cour, dec, stren, listed, owner, grad, pres,
           state, saved, image, outgoing, incoming,
           load_sem, halo_send, halo_recv, block_send, block_recv, pres_sem):
    emit = lax.axis_index("emit")
    vx = lax.axis_index("vx")
    vy = lax.axis_index("vy")
    other = 1 - vy
    per = outgoing.shape[1]
    end = TOP + rows
    has_low = vx > 0
    has_high = vx < n_vx - 1

    loads = []
    for j in range(2):
        cut = pl.ds(j * BC, BC)
        place = pl.ds(TOP, rows)
        pairs = [(fwd.at[:, 0, :, cut], state.at[pl.ds(0, 3), j, place, :]),
                 (adj.at[:, 0, :, cut], state.at[pl.ds(3, 3), j, place, :])]
        for at, ref in enumerate((cour, dec, stren)):
            pairs.append((ref.at[:, cut], state.at[6 + at, j, place, :]))
        for source, target in pairs:
            copy = pltpu.make_async_copy(source, target, load_sem.at[len(loads)])
            copy.start()
            loads.append(copy)

    barrier = pltpu.get_barrier_semaphore()

    def greet(where):
        pl.semaphore_signal(barrier, inc=1, device_id=where, device_id_type=MESH)

    greet((emit, vx, other))

    @pl.when(has_low)
    def _():
        greet((emit, vx - 1, vy))
        greet((emit, vx - 1, other))

    @pl.when(has_high)
    def _():
        greet((emit, vx + 1, vy))
        greet((emit, vx + 1, other))

    for step in range(1, n_emit):
        greet((lax.rem(emit + step, n_emit), vx, vy))

    blank = jnp.zeros((HALO, BC), jnp.float32)

    @pl.when(vx == 0)
    def _():
        for field in range(9):
            for j in range(3):
                state[field, j, pl.ds(TOP - HALO, HALO), :] = blank

    @pl.when(vx == n_vx - 1)
    def _():
        for field in range(9):
            for j in range(3):
                state[field, j, pl.ds(end, HALO), :] = blank

    bits = jnp.int32(0)
    for at in range(listed.shape[-1]):
        bits = bits | lax.shift_left(jnp.int32(1), listed[0, 0, 0, at])

    for copy in loads:
        copy.wait()
    near = (vx > 0).astype(jnp.int32) + (vx < n_vx - 1).astype(jnp.int32)
    pl.semaphore_wait(barrier, n_emit + 2 * near)

    def remote(source, target, at, where):
        return pltpu.make_async_remote_copy(
            src_ref=source, dst_ref=target, send_sem=halo_send.at[at],
            recv_sem=halo_recv.at[at], device_id=where, device_id_type=MESH)

    side = remote(state.at[:, other, pl.ds(TOP, rows), :], state.at[:, 2, pl.ds(TOP, rows), :],
                  2, (emit, vx, other))
    first = pl.ds(TOP, HALO)
    last = pl.ds(end - HALO, HALO)
    above = pl.ds(TOP - HALO, HALO)
    below = pl.ds(end, HALO)
    pair = pl.ds(0, 2)

    def to_high():
        return (remote(state.at[:, pair, last, :], state.at[:, pair, above, :], 0, (emit, vx + 1, vy)),
                remote(state.at[:, other, last, :], state.at[:, 2, above, :], 3, (emit, vx + 1, other)))

    def to_low():
        return (remote(state.at[:, pair, first, :], state.at[:, pair, below, :], 1, (emit, vx - 1, vy)),
                remote(state.at[:, other, first, :], state.at[:, 2, below, :], 4, (emit, vx - 1, other)))

    @pl.when(has_high)
    def _():
        for copy in to_high():
            copy.start()

    @pl.when(has_low)
    def _():
        for copy in to_low():
            copy.start()

    side.start()

    @pl.when(has_high)
    def _():
        for copy in to_high():
            copy.wait_send()
        for copy in to_low():
            copy.wait_recv()

    @pl.when(has_low)
    def _():
        for copy in to_low():
            copy.wait_send()
        for copy in to_high():
            copy.wait_recv()

    side.wait_send()
    side.wait_recv()

    lane = lax.broadcasted_iota(jnp.int32, (CHUNK, BC), 1)
    east_on = (1 - vy).astype(jnp.float32)
    west_on = vy.astype(jnp.float32)

    def advance(base, number, row, count, cols):
        now = base + number % 2
        new = base + (number + 1) % 2
        center, curves = laplace_rows(state, now, row, count, cols, lane, east_on, west_on)
        place = pl.ds(row, count)
        seconds, fields = [], []
        for j in range(cols):
            memory = state[7, j, place, :] * state[base + 2, j, place, :] + state[8, j, place, :] * curves[j]
            second = state[6, j, place, :] * (curves[j] - memory)
            following = (2.0 * center[j] - state[new, j, place, :]) + second
            if number < STEPS:
                state[base + 2, j, place, :] = memory
            state[new, j, place, :] = following
            seconds.append(second)
            fields.append(following)
        return seconds, fields

    def step_body(number):
        def body(at, carry):
            row = TOP - HALO + at * CHUNK
            seconds, _ = advance(0, number, row, CHUNK, 3)
            _, fields = advance(3, number, row, CHUNK, 3)
            place = pl.ds(row, CHUNK)
            for j in range(2):
                if number == 1:
                    saved[0, j, place, :] = seconds[j]
                    saved[1, j, place, :] = fields[j]
                elif number == 2:
                    saved[2, j, place, :] = seconds[j]
                    saved[3, j, place, :] = fields[j]
                else:
                    saved[2, j, place, :] = (seconds[j] * saved[3, j, place, :]
                                             + fields[j] * saved[2, j, place, :])
            return carry
        return body

    for number in range(1, STEPS):
        lax.fori_loop(0, (rows + 2 * HALO) // CHUNK, step_body(number), 0)

    def last_body(at, carry):
        row = TOP + at * CHUNK
        seconds, _ = advance(0, STEPS, row, CHUNK, 2)
        _, fields = advance(3, STEPS, row, CHUNK, 2)
        place = pl.ds(row, CHUNK)
        for j in range(2):
            total = (saved[2, j, place, :] + saved[0, j, place, :] * fields[j]
                     + saved[1, j, place, :] * seconds[j])
            image[at * 2 + j] = total * (1.0 / n_emit)
        return carry

    lax.fori_loop(0, rows // CHUNK, last_body, 0)

    pres_copies = []
    for j in range(2):
        copy = pltpu.make_async_copy(state.at[(STEPS + 1) % 2, j, pl.ds(TOP, rows), :],
                                     pres.at[0, :, pl.ds(j * BC, BC)], pres_sem.at[j])
        copy.start()
        pres_copies.append(copy)

    def masked(slot):
        block = owner[0, 0, slot]
        hit = (lax.shift_right_logical(bits, block) & 1).astype(jnp.float32)
        return image[block] * hit

    def exchange(peer):
        return pltpu.make_async_remote_copy(
            src_ref=outgoing.at[peer], dst_ref=incoming.at[emit], send_sem=block_send.at[peer],
            recv_sem=block_recv.at[emit], device_id=(peer, vx, vy), device_id_type=MESH)

    for step in range(1, n_emit):
        peer = lax.rem(emit + step, n_emit)
        for at in range(per):
            outgoing[peer, at] = masked(peer * per + at)
        exchange(peer).start()

    for at in range(per):
        incoming[emit, at] = masked(emit * per + at)

    for step in range(1, n_emit):
        peer = lax.rem(emit + step, n_emit)
        pltpu.make_async_remote_copy(
            src_ref=outgoing.at[peer], dst_ref=incoming.at[peer], send_sem=block_send.at[peer],
            recv_sem=block_recv.at[peer], device_id=(peer, vx, vy), device_id_type=MESH).wait()

    for at in range(per):
        total = incoming[0, at]
        for source in range(1, n_emit):
            total = total + incoming[source, at]
        grad[at] = total
    for copy in pres_copies:
        copy.wait()


def shards(n_emit, n_vx, fwd_state, adj_state, courant, decay_rate, strength, footprint, owner_map):
    rows = fwd_state.shape[2]
    blocks = owner_map.shape[-1]
    per = blocks // n_emit
    padded = rows + 2 * TOP
    anywhere = pl.BlockSpec(memory_space=pl.ANY)
    scalars = pl.BlockSpec(memory_space=pltpu.SMEM)
    return pl.pallas_call(
        functools.partial(kernel, n_emit, n_vx, rows),
        out_shape=(jax.ShapeDtypeStruct((per, BR, BC), jnp.float32),
                   jax.ShapeDtypeStruct((1, rows, 2 * BC), jnp.float32)),
        in_specs=[anywhere] * 5 + [scalars] * 2,
        out_specs=(pl.BlockSpec(memory_space=pltpu.VMEM), anywhere),
        scratch_shapes=[
            pltpu.VMEM((9, 3, padded, BC), jnp.float32),
            pltpu.VMEM((4, 2, padded, BC), jnp.float32),
            pltpu.VMEM((blocks, BR, BC), jnp.float32),
            pltpu.VMEM((n_emit, per, BR, BC), jnp.float32),
            pltpu.VMEM((n_emit, per, BR, BC), jnp.float32),
            pltpu.SemaphoreType.DMA((10,)),
            pltpu.SemaphoreType.DMA((5,)),
            pltpu.SemaphoreType.DMA((5,)),
            pltpu.SemaphoreType.DMA((n_emit,)),
            pltpu.SemaphoreType.DMA((n_emit,)),
            pltpu.SemaphoreType.DMA((2,)),
        ],
        compiler_params=pltpu.CompilerParams(collective_id=0, has_side_effects=True),
        name="waves",
    )(fwd_state, adj_state, courant, decay_rate, strength, footprint, owner_map)


def solution(mesh):
    in_specs = (
        P(None, "emit", "vx", "vy"),
        P(None, "emit", "vx", "vy"),
        P("vx", "vy"),
        P("vx", "vy"),
        P("vx", "vy"),
        P("emit", "vx", "vy", None),
        P("vx", "vy", None),
    )
    out_specs = (P("emit", "vx", "vy"), P("emit", "vx", "vy"))
    body = functools.partial(shards, mesh.shape["emit"], mesh.shape["vx"])
    return jax.shard_map(body, mesh=mesh, in_specs=in_specs, out_specs=out_specs, check_vma=False)
```

```python
import functools

import jax
import jax.numpy as jnp
from jax import lax
from jax.experimental import pallas as pl
from jax.experimental.pallas import tpu as pltpu
from jax.sharding import PartitionSpec as P

BR = 16
BC = 128
STEPS = 4
TOP = 16
HALO = 8
CHUNK = 16
MESH = pl.DeviceIdType.MESH


def laplace_rows(state, field, row, count, cols, lane, east_on, west_on):
    center = [state[field, j, pl.ds(row, count), :] for j in range(3)]
    east = [pltpu.roll(center[j], BC - 1, 1) for j in range(3)]
    west = [pltpu.roll(center[j], 1, 1) for j in range(3)]
    curves = []
    for j in range(cols):
        after = east[(j + 1) % 3]
        before = west[(j + 2) % 3]
        if j == 1:
            after = after * east_on
        if j == 0:
            before = before * west_on
        right = jnp.where(lane == BC - 1, after, east[j])
        left = jnp.where(lane == 0, before, west[j])
        up = state[field, j, pl.ds(row - 1, count), :]
        down = state[field, j, pl.ds(row + 1, count), :]
        curves.append((up + down) + (left + right) - 4.0 * center[j])
    return center, curves


def kernel(n_emit, n_vx, rows, fwd, adj, cour, dec, stren, listed, owner, grad, pres,
           state, saved, outgoing, incoming,
           load_sem, halo_send, halo_recv, block_send, block_recv, pres_sem):
    emit = lax.axis_index("emit")
    vx = lax.axis_index("vx")
    vy = lax.axis_index("vy")
    other = 1 - vy
    per = outgoing.shape[1]
    end = TOP + rows
    has_low = vx > 0
    has_high = vx < n_vx - 1

    loads = []
    for j in range(2):
        cut = pl.ds(j * BC, BC)
        place = pl.ds(TOP, rows)
        pairs = [(fwd.at[:, 0, :, cut], state.at[pl.ds(0, 3), j, place, :]),
                 (adj.at[:, 0, :, cut], state.at[pl.ds(3, 3), j, place, :])]
        for at, ref in enumerate((cour, dec, stren)):
            pairs.append((ref.at[:, cut], state.at[6 + at, j, place, :]))
        for source, target in pairs:
            copy = pltpu.make_async_copy(source, target, load_sem.at[len(loads)])
            copy.start()
            loads.append(copy)

    barrier = pltpu.get_barrier_semaphore()

    def greet(where):
        pl.semaphore_signal(barrier, inc=1, device_id=where, device_id_type=MESH)

    greet((emit, vx, other))

    @pl.when(has_low)
    def _():
        greet((emit, vx - 1, vy))
        greet((emit, vx - 1, other))

    @pl.when(has_high)
    def _():
        greet((emit, vx + 1, vy))
        greet((emit, vx + 1, other))

    for step in range(1, n_emit):
        greet((lax.rem(emit + step, n_emit), vx, vy))

    blank = jnp.zeros((HALO, BC), jnp.float32)

    @pl.when(vx == 0)
    def _():
        for field in range(9):
            for j in range(3):
                state[field, j, pl.ds(TOP - HALO, HALO), :] = blank

    @pl.when(vx == n_vx - 1)
    def _():
        for field in range(9):
            for j in range(3):
                state[field, j, pl.ds(end, HALO), :] = blank

    bits = jnp.int32(0)
    for at in range(listed.shape[-1]):
        bits = bits | lax.shift_left(jnp.int32(1), listed[0, 0, 0, at])

    for copy in loads:
        copy.wait()
    near = (vx > 0).astype(jnp.int32) + (vx < n_vx - 1).astype(jnp.int32)
    pl.semaphore_wait(barrier, n_emit + 2 * near)

    def remote(source, target, at, where):
        return pltpu.make_async_remote_copy(
            src_ref=source, dst_ref=target, send_sem=halo_send.at[at],
            recv_sem=halo_recv.at[at], device_id=where, device_id_type=MESH)

    side = remote(state.at[:, other, pl.ds(TOP, rows), :], state.at[:, 2, pl.ds(TOP, rows), :],
                  2, (emit, vx, other))
    first = pl.ds(TOP, HALO)
    last = pl.ds(end - HALO, HALO)
    above = pl.ds(TOP - HALO, HALO)
    below = pl.ds(end, HALO)
    pair = pl.ds(0, 2)

    def to_high():
        return (remote(state.at[:, pair, last, :], state.at[:, pair, above, :], 0, (emit, vx + 1, vy)),
                remote(state.at[:, other, last, :], state.at[:, 2, above, :], 3, (emit, vx + 1, other)))

    def to_low():
        return (remote(state.at[:, pair, first, :], state.at[:, pair, below, :], 1, (emit, vx - 1, vy)),
                remote(state.at[:, other, first, :], state.at[:, 2, below, :], 4, (emit, vx - 1, other)))

    @pl.when(has_high)
    def _():
        for copy in to_high():
            copy.start()

    @pl.when(has_low)
    def _():
        for copy in to_low():
            copy.start()

    side.start()

    @pl.when(has_high)
    def _():
        for copy in to_high():
            copy.wait_send()
        for copy in to_low():
            copy.wait_recv()

    @pl.when(has_low)
    def _():
        for copy in to_low():
            copy.wait_send()
        for copy in to_high():
            copy.wait_recv()

    side.wait_send()
    side.wait_recv()

    lane = lax.broadcasted_iota(jnp.int32, (CHUNK, BC), 1)
    east_on = (1 - vy).astype(jnp.float32)
    west_on = vy.astype(jnp.float32)

    def update(field, base, number, cols, place):
        center, curves, col = field
        now_before = base + (number + 1) % 2
        results = []
        for j in range(cols):
            memory = state[7, col[j], place, :] * state[base + 2, col[j], place, :] + state[8, col[j], place, :] * curves[j]
            second = state[6, col[j], place, :] * (curves[j] - memory)
            following = (2.0 * center[j] - state[now_before, col[j], place, :]) + second
            results.append((memory, second, following))
        return results

    def advance(base, number, row, count, cols):
        center, curves = laplace_rows(state, base + number % 2, row, count, cols, lane, east_on, west_on)
        return update((center, curves, range(cols)), base, number, cols, pl.ds(row, count))

    def step_body(number):
        new = (number + 1) % 2

        def body(at, carry):
            row = TOP - HALO + at * CHUNK
            forward = advance(0, number, row, CHUNK, 3)
            adjoint = advance(3, number, row, CHUNK, 3)
            place = pl.ds(row, CHUNK)
            if number == 3:
                partial = [forward[j][1] * saved[3, j, place, :] + adjoint[j][2] * saved[2, j, place, :]
                           for j in range(2)]
            for j in range(3):
                for base, result in ((0, forward), (3, adjoint)):
                    state[base + 2, j, place, :] = result[j][0]
                    state[base + new, j, place, :] = result[j][2]
            for j in range(2):
                if number < 3:
                    saved[2 * number - 2, j, place, :] = forward[j][1]
                    saved[2 * number - 1, j, place, :] = adjoint[j][2]
                else:
                    saved[2, j, place, :] = partial[j]
            return carry
        return body

    for number in range(1, STEPS):
        lax.fori_loop(0, (rows + 2 * HALO) // CHUNK, step_body(number), 0)

    def block_step(base, block, row):
        now = base + STEPS % 2
        col = block & 1
        after_col = col + 1
        before_col = jnp.where(col == 0, 2, 0)
        after_on = jnp.where(col == 1, east_on, 1.0)
        before_on = jnp.where(col == 0, west_on, 1.0)
        place = pl.ds(row, BR)
        center = state[now, col, place, :]
        after = pltpu.roll(state[now, after_col, place, :], BC - 1, 1) * after_on
        before = pltpu.roll(state[now, before_col, place, :], 1, 1) * before_on
        right = jnp.where(lane == BC - 1, after, pltpu.roll(center, BC - 1, 1))
        left = jnp.where(lane == 0, before, pltpu.roll(center, 1, 1))
        up = state[now, col, pl.ds(row - 1, BR), :]
        down = state[now, col, pl.ds(row + 1, BR), :]
        curve = (up + down) + (left + right) - 4.0 * center
        return update(([center], [curve], [col]), base, STEPS, 1, place)[0]

    def masked(slot):
        block = owner[0, 0, slot]
        row = TOP + lax.shift_right_logical(block, 1) * BR
        col = block & 1
        hit = (lax.shift_right_logical(bits, block) & 1).astype(jnp.float32)
        _, second, _ = block_step(0, block, row)
        _, _, field = block_step(3, block, row)
        place = pl.ds(row, BR)
        total = (saved[2, col, place, :] + saved[0, col, place, :] * field
                 + saved[1, col, place, :] * second)
        return total * (hit * (1.0 / n_emit))

    def exchange(peer, slot):
        return pltpu.make_async_remote_copy(
            src_ref=outgoing.at[peer], dst_ref=incoming.at[slot], send_sem=block_send.at[peer],
            recv_sem=block_recv.at[slot], device_id=(peer, vx, vy), device_id_type=MESH)

    def send_body(step, carry):
        peer = lax.rem(emit + step, n_emit)
        parts = [masked(peer * per + at) for at in range(per)]
        for at in range(per):
            outgoing[peer, at] = parts[at]
        exchange(peer, emit).start()
        return carry

    lax.fori_loop(1, n_emit, send_body, 0)
    parts = [masked(emit * per + at) for at in range(per)]
    for at in range(per):
        incoming[emit, at] = parts[at]

    def last_body(at, carry):
        row = TOP + at * CHUNK
        forward = advance(0, STEPS, row, CHUNK, 2)
        for j in range(2):
            state[(STEPS + 1) % 2, j, pl.ds(row, CHUNK), :] = forward[j][2]
        return carry

    lax.fori_loop(0, rows // CHUNK, last_body, 0)

    pres_copies = []
    for j in range(2):
        copy = pltpu.make_async_copy(state.at[(STEPS + 1) % 2, j, pl.ds(TOP, rows), :],
                                     pres.at[0, :, pl.ds(j * BC, BC)], pres_sem.at[j])
        copy.start()
        pres_copies.append(copy)

    for step in range(1, n_emit):
        peer = lax.rem(emit + step, n_emit)
        exchange(peer, peer).wait()

    for at in range(per):
        total = incoming[0, at]
        for source in range(1, n_emit):
            total = total + incoming[source, at]
        grad[at] = total
    for copy in pres_copies:
        copy.wait()


def hand_over(found, waves, grad, pres, sem):
    copies = [pltpu.make_async_copy(waves, pres, sem.at[0]),
              pltpu.make_async_copy(found, grad, sem.at[1])]
    for copy in copies:
        copy.start()
    for copy in copies:
        copy.wait()


def shards(n_emit, n_vx, fwd_state, adj_state, courant, decay_rate, strength, footprint, owner_map):
    rows = fwd_state.shape[2]
    blocks = owner_map.shape[-1]
    per = blocks // n_emit
    padded = rows + 2 * TOP
    anywhere = pl.BlockSpec(memory_space=pl.ANY)
    scalars = pl.BlockSpec(memory_space=pltpu.SMEM)
    found, waves = pl.pallas_call(
        functools.partial(kernel, n_emit, n_vx, rows),
        out_shape=(jax.ShapeDtypeStruct((per, BR, BC), jnp.float32),
                   jax.ShapeDtypeStruct((1, rows, 2 * BC), jnp.float32)),
        in_specs=[anywhere] * 5 + [scalars] * 2,
        out_specs=(pl.BlockSpec(memory_space=pltpu.VMEM), anywhere),
        scratch_shapes=[
            pltpu.VMEM((9, 3, padded, BC), jnp.float32),
            pltpu.VMEM((4, 2, padded, BC), jnp.float32),
            pltpu.VMEM((n_emit, per, BR, BC), jnp.float32),
            pltpu.VMEM((n_emit, per, BR, BC), jnp.float32),
            pltpu.SemaphoreType.DMA((10,)),
            pltpu.SemaphoreType.DMA((5,)),
            pltpu.SemaphoreType.DMA((5,)),
            pltpu.SemaphoreType.DMA((n_emit,)),
            pltpu.SemaphoreType.DMA((n_emit,)),
            pltpu.SemaphoreType.DMA((2,)),
        ],
        compiler_params=pltpu.CompilerParams(collective_id=0, has_side_effects=True),
        name="waves",
    )(fwd_state, adj_state, courant, decay_rate, strength, footprint, owner_map)
    return pl.pallas_call(
        hand_over,
        out_shape=(jax.ShapeDtypeStruct(found.shape, jnp.float32),
                   jax.ShapeDtypeStruct(waves.shape, jnp.float32)),
        in_specs=[anywhere] * 2,
        out_specs=(anywhere, anywhere),
        scratch_shapes=[pltpu.SemaphoreType.DMA((2,))],
        name="hand_over",
    )(found, waves)


def solution(mesh):
    in_specs = (
        P(None, "emit", "vx", "vy"),
        P(None, "emit", "vx", "vy"),
        P("vx", "vy"),
        P("vx", "vy"),
        P("vx", "vy"),
        P("emit", "vx", "vy", None),
        P("vx", "vy", None),
    )
    out_specs = (P("emit", "vx", "vy"), P("emit", "vx", "vy"))
    body = functools.partial(shards, mesh.shape["emit"], mesh.shape["vx"])
    return jax.shard_map(body, mesh=mesh, in_specs=in_specs, out_specs=out_specs, check_vma=False)
```

```python
import functools

import jax
import jax.numpy as jnp
from jax import lax
from jax.experimental import pallas as pl
from jax.experimental.pallas import tpu as pltpu
from jax.sharding import PartitionSpec as P

BR = 16
BC = 128
STEPS = 4
WIDE = 4
TOP = 16
HALO = 8
CHUNK = 32
ARRAYS = 9
MESH = pl.DeviceIdType.MESH


def lanes(count):
    return lax.broadcasted_iota(jnp.int32, (count, BC), 1)


def kernel(n_emit, n_vx, rows, fwd, adj, cour, dec, stren, listed, owner, grad, pres,
           *scratch):
    state = scratch[:ARRAYS]
    (saved, rowsend, rowrecv, colsend, colrecv, first_out, first_in, own_part, second_out, second_in,
     load_sem, halo_send, halo_recv, first_send, first_recv, second_send, second_recv,
     pres_sem) = scratch[ARRAYS:]
    courant, decay, strength = state[6:]
    emit = lax.axis_index("emit")
    vx = lax.axis_index("vx")
    vy = lax.axis_index("vy")
    other = 1 - vy
    half = n_emit // 2
    parity = lax.rem(emit, 2)
    line = emit // 2
    partner = emit + 1 - 2 * parity
    per = second_in.shape[1]
    end = TOP + rows
    has_low = vx > 0
    has_high = vx < n_vx - 1

    sources = [fwd.at[at, 0] for at in range(3)] + [adj.at[at, 0] for at in range(3)] + [cour, dec, stren]
    loads = []
    for col in (other, vy):
        cut = pl.ds(pl.multiple_of(col * BC, BC), BC)
        for at in range(ARRAYS):
            copy = pltpu.make_async_copy(sources[at].at[:, cut], state[at].at[col, pl.ds(TOP, rows), :],
                                         load_sem.at[len(loads)])
            copy.start()
            loads.append(copy)

    barrier = pltpu.get_barrier_semaphore()

    def greet(where):
        pl.semaphore_signal(barrier, inc=1, device_id=where, device_id_type=MESH)

    greet((emit, vx, other))

    @pl.when(has_low)
    def _():
        greet((emit, vx - 1, vy))
        greet((emit, vx - 1, other))

    @pl.when(has_high)
    def _():
        greet((emit, vx + 1, vy))
        greet((emit, vx + 1, other))

    greet((partner, vx, vy))
    for step in range(1, half):
        greet((2 * lax.rem(line + step, half) + parity, vx, vy))

    @pl.when(vx == 0)
    def _():
        rowrecv[0] = jnp.zeros(rowrecv.shape[1:], jnp.float32)
        colrecv[pl.ds(0, HALO), :] = jnp.zeros((HALO, BC), jnp.float32)

    @pl.when(vx == n_vx - 1)
    def _():
        rowrecv[1] = jnp.zeros(rowrecv.shape[1:], jnp.float32)
        colrecv[pl.ds(HALO + rows, HALO), :] = jnp.zeros((HALO, BC), jnp.float32)

    bits = jnp.int32(0)
    for at in range(listed.shape[-1]):
        bits = bits | lax.shift_left(jnp.int32(1), listed[0, 0, 0, at])

    for copy in loads[:ARRAYS]:
        copy.wait()
    base = other * (BC - WIDE)
    group = lax.rem(lanes(CHUNK) + (BC - base), BC) // WIDE

    def pack(at, carry):
        row = at * CHUNK
        packed = state[0][other, pl.ds(TOP + row, CHUNK), :]
        for which in range(1, ARRAYS):
            moved = pltpu.roll(state[which][other, pl.ds(TOP + row, CHUNK), :], WIDE * which, 1)
            packed = jnp.where(group == which, moved, packed)
        colsend[pl.ds(row, CHUNK), :] = packed
        return carry

    lax.fori_loop(0, rows // CHUNK, pack, 0)
    for copy in loads[ARRAYS:]:
        copy.wait()
    for which in range(ARRAYS):
        for col in range(2):
            place = pl.ds(WIDE * which, WIDE)
            rowsend[0, col, place, :] = state[which][col, pl.ds(TOP, WIDE), :]
            rowsend[1, col, place, :] = state[which][col, pl.ds(end - WIDE, WIDE), :]

    near = (vx > 0).astype(jnp.int32) + (vx < n_vx - 1).astype(jnp.int32)
    pl.semaphore_wait(barrier, half + 1 + 2 * near)

    def remote(source, target, at, where):
        return pltpu.make_async_remote_copy(
            src_ref=source, dst_ref=target, send_sem=halo_send.at[at],
            recv_sem=halo_recv.at[at], device_id=where, device_id_type=MESH)

    side = remote(colsend, colrecv.at[pl.ds(HALO, rows), :], 2, (emit, vx, other))

    def to_high():
        return (remote(rowsend.at[1], rowrecv.at[0], 0, (emit, vx + 1, vy)),
                remote(colsend.at[pl.ds(rows - HALO, HALO), :], colrecv.at[pl.ds(0, HALO), :], 3,
                       (emit, vx + 1, other)))

    def to_low():
        return (remote(rowsend.at[0], rowrecv.at[1], 1, (emit, vx - 1, vy)),
                remote(colsend.at[pl.ds(0, HALO), :], colrecv.at[pl.ds(HALO + rows, HALO), :], 4,
                       (emit, vx - 1, other)))

    @pl.when(has_high)
    def _():
        for copy in to_high():
            copy.start()

    @pl.when(has_low)
    def _():
        for copy in to_low():
            copy.start()

    side.start()

    @pl.when(has_high)
    def _():
        for copy in to_low():
            copy.wait_recv()

    @pl.when(has_low)
    def _():
        for copy in to_high():
            copy.wait_recv()

    side.wait_recv()

    unpack_rows = (rows + 2 * HALO) // 2

    def unpack(at, carry):
        packed = colrecv[pl.ds(at * unpack_rows, unpack_rows), :]
        for which in range(ARRAYS):
            moved = packed if which == 0 else pltpu.roll(packed, BC - WIDE * which, 1)
            state[which][2, pl.ds(TOP - HALO + at * unpack_rows, unpack_rows), :] = moved
        return carry

    lax.fori_loop(0, 2, unpack, 0)
    for which in range(ARRAYS):
        for col in range(2):
            place = pl.ds(WIDE * which, WIDE)
            state[which][col, pl.ds(TOP - WIDE, WIDE), :] = rowrecv[0, col, place, :]
            state[which][col, pl.ds(end, WIDE), :] = rowrecv[1, col, place, :]

    east_on = (1 - vy).astype(jnp.float32)
    west_on = vy.astype(jnp.float32)

    def laplace_rows(field, row, count, cols):
        lane = lanes(count)
        center = [field[j, pl.ds(row, count), :] for j in range(3)]
        east = [pltpu.roll(center[j], BC - 1, 1) for j in range(3)]
        west = [pltpu.roll(center[j], 1, 1) for j in range(3)]
        curves = []
        for j in range(cols):
            after = east[(j + 1) % 3]
            before = west[(j + 2) % 3]
            if j == 1:
                after = after * east_on
            if j == 0:
                before = before * west_on
            right = jnp.where(lane == BC - 1, after, east[j])
            left = jnp.where(lane == 0, before, west[j])
            up = field[j, pl.ds(row - 1, count), :]
            down = field[j, pl.ds(row + 1, count), :]
            curves.append((up + down) + (left + right) - 4.0 * center[j])
        return center, curves

    def update(base, number, col, place, center, curve):
        memory = decay[col, place, :] * state[base + 2][col, place, :] + strength[col, place, :] * curve
        second = courant[col, place, :] * (curve - memory)
        following = (2.0 * center - state[base + (number + 1) % 2][col, place, :]) + second
        return memory, second, following

    def advance(base, number, row, count, cols):
        center, curves = laplace_rows(state[base + number % 2], row, count, cols)
        return [update(base, number, j, pl.ds(row, count), center[j], curves[j]) for j in range(cols)]

    def step_rows(number, row, count, keep):
        place = pl.ds(row, count)
        new = (number + 1) % 2
        results = []
        for base in (0, 3):
            result = advance(base, number, row, count, 3)
            for j in range(3):
                state[base + 2][j, place, :] = result[j][0]
                state[base + new][j, place, :] = result[j][2]
            results.append(result)
        if not keep:
            return
        forward, adjoint = results
        for j in range(2):
            if number < 3:
                saved[2 * number - 2, j, place, :] = forward[j][1]
                saved[2 * number - 1, j, place, :] = adjoint[j][2]
            else:
                saved[2, j, place, :] = (forward[j][1] * saved[3, j, place, :]
                                         + adjoint[j][2] * saved[2, j, place, :])

    for number in range(1, STEPS):
        def body(at, carry, number=number):
            step_rows(number, TOP + at * CHUNK, CHUNK, True)
            return carry

        lax.fori_loop(0, rows // CHUNK, body, 0)
        step_rows(number, TOP - HALO, HALO, False)
        step_rows(number, end, HALO, False)

    lane = lanes(BR)

    def block_step(base, block, row):
        field = state[base + STEPS % 2]
        col = block & 1
        before_col = jnp.where(col == 0, 2, 0)
        after_on = jnp.where(col == 1, east_on, 1.0)
        before_on = jnp.where(col == 0, west_on, 1.0)
        place = pl.ds(row, BR)
        center = field[col, place, :]
        after = pltpu.roll(field[col + 1, place, :], BC - 1, 1) * after_on
        before = pltpu.roll(field[before_col, place, :], 1, 1) * before_on
        right = jnp.where(lane == BC - 1, after, pltpu.roll(center, BC - 1, 1))
        left = jnp.where(lane == 0, before, pltpu.roll(center, 1, 1))
        up = field[col, pl.ds(row - 1, BR), :]
        down = field[col, pl.ds(row + 1, BR), :]
        curve = (up + down) + (left + right) - 4.0 * center
        return update(base, STEPS, col, place, center, curve)

    def masked(slot):
        block = owner[0, 0, slot]
        row = TOP + lax.shift_right_logical(block, 1) * BR
        col = block & 1
        hit = (lax.shift_right_logical(bits, block) & 1).astype(jnp.float32)
        _, second, _ = block_step(0, block, row)
        _, _, field = block_step(3, block, row)
        place = pl.ds(row, BR)
        total = (saved[2, col, place, :] + saved[0, col, place, :] * field
                 + saved[1, col, place, :] * second)
        return total * (hit * (1.0 / n_emit))

    def to_partner(at):
        return pltpu.make_async_remote_copy(
            src_ref=first_out.at[at], dst_ref=first_in.at[at], send_sem=first_send.at[at],
            recv_sem=first_recv.at[at], device_id=(partner, vx, vy), device_id_type=MESH)

    def to_owner(at, slot):
        return pltpu.make_async_remote_copy(
            src_ref=second_out.at[at], dst_ref=second_in.at[slot], send_sem=second_send.at[at],
            recv_sem=second_recv.at[slot], device_id=(2 * at + parity, vx, vy), device_id_type=MESH)

    offsets = [half // 2 + at for at in range(half - half // 2)] + list(range(1, half // 2)) + [0]
    order = [lax.rem(line + offset, half) for offset in offsets]

    for at in order:
        parts = [masked((2 * at + 1 - parity) * per + slot) for slot in range(per)]
        for slot in range(per):
            first_out[at, slot] = parts[slot]
        to_partner(at).start()
    for at in order:
        parts = [masked((2 * at + parity) * per + slot) for slot in range(per)]
        for slot in range(per):
            own_part[at, slot] = parts[slot]
    for at in order[:-1]:
        to_partner(at).wait_recv()
        second_out[at] = own_part[at] + first_in[at]
        to_owner(at, line).start()
    to_partner(line).wait_recv()
    second_in[line] = own_part[line] + first_in[line]

    def last_body(at, carry):
        row = TOP + at * CHUNK
        forward = advance(0, STEPS, row, CHUNK, 2)
        for j in range(2):
            state[(STEPS + 1) % 2][j, pl.ds(row, CHUNK), :] = forward[j][2]
        return carry

    lax.fori_loop(0, rows // CHUNK, last_body, 0)

    pres_copies = []
    for j in range(2):
        copy = pltpu.make_async_copy(state[(STEPS + 1) % 2].at[j, pl.ds(TOP, rows), :],
                                     pres.at[0, :, pl.ds(j * BC, BC)], pres_sem.at[j])
        copy.start()
        pres_copies.append(copy)

    side.wait_send()

    @pl.when(has_high)
    def _():
        for copy in to_high():
            copy.wait_send()

    @pl.when(has_low)
    def _():
        for copy in to_low():
            copy.wait_send()

    for at in range(half):
        to_partner(at).wait_send()
    for at in order[:-1]:
        to_owner(at, at).wait()
    total = second_in[0]
    for at in range(1, half):
        total = total + second_in[at]
    grad[...] = total
    for copy in pres_copies:
        copy.wait()


def hand_over(found, waves, grad, pres, found_here, waves_here, sem):
    parts = 4
    rows = waves.shape[1] // parts
    steps = [(found, found_here, grad)]
    for at in range(parts):
        place = pl.ds(at * rows, rows)
        steps.append((waves.at[:, place, :], waves_here.at[:, place, :], pres.at[:, place, :]))
    taken = [pltpu.make_async_copy(source, here, sem.at[0, at]) for at, (source, here, _) in enumerate(steps)]
    given = [pltpu.make_async_copy(here, target, sem.at[1, at]) for at, (_, here, target) in enumerate(steps)]
    for copy in taken:
        copy.start()
    for into, out in zip(taken, given):
        into.wait()
        out.start()
    for copy in given:
        copy.wait()


def shards(n_emit, n_vx, fwd_state, adj_state, courant, decay_rate, strength, footprint, owner_map):
    rows = fwd_state.shape[2]
    blocks = owner_map.shape[-1]
    per = blocks // n_emit
    half = n_emit // 2
    padded = rows + 2 * TOP
    anywhere = pl.BlockSpec(memory_space=pl.ANY)
    scalars = pl.BlockSpec(memory_space=pltpu.SMEM)

    def blocks_of(count):
        return pltpu.VMEM((count, per, BR, BC), jnp.float32)

    found, waves = pl.pallas_call(
        functools.partial(kernel, n_emit, n_vx, rows),
        out_shape=(jax.ShapeDtypeStruct((per, BR, BC), jnp.float32),
                   jax.ShapeDtypeStruct((1, rows, 2 * BC), jnp.float32)),
        in_specs=[anywhere] * 5 + [scalars] * 2,
        out_specs=(pl.BlockSpec(memory_space=pltpu.VMEM), anywhere),
        scratch_shapes=[pltpu.VMEM((3, padded, BC), jnp.float32)] * ARRAYS + [
            pltpu.VMEM((4, 2, padded, BC), jnp.float32),
            pltpu.VMEM((2, 2, 40, BC), jnp.float32),
            pltpu.VMEM((2, 2, 40, BC), jnp.float32),
            pltpu.VMEM((rows, BC), jnp.float32),
            pltpu.VMEM((rows + 2 * HALO, BC), jnp.float32),
        ] + [blocks_of(half)] * 5 + [
            pltpu.SemaphoreType.DMA((2 * ARRAYS,)),
            pltpu.SemaphoreType.DMA((5,)),
            pltpu.SemaphoreType.DMA((5,)),
            pltpu.SemaphoreType.DMA((half,)),
            pltpu.SemaphoreType.DMA((half,)),
            pltpu.SemaphoreType.DMA((half,)),
            pltpu.SemaphoreType.DMA((half,)),
            pltpu.SemaphoreType.DMA((2,)),
        ],
        compiler_params=pltpu.CompilerParams(collective_id=0, has_side_effects=True),
        name="waves",
    )(fwd_state, adj_state, courant, decay_rate, strength, footprint, owner_map)
    return pl.pallas_call(
        hand_over,
        out_shape=(jax.ShapeDtypeStruct(found.shape, jnp.float32),
                   jax.ShapeDtypeStruct(waves.shape, jnp.float32)),
        in_specs=[anywhere] * 2,
        out_specs=(anywhere, anywhere),
        scratch_shapes=[pltpu.VMEM(found.shape, jnp.float32), pltpu.VMEM(waves.shape, jnp.float32),
                        pltpu.SemaphoreType.DMA((2, 5))],
        name="hand_over",
    )(found, waves)


def solution(mesh):
    in_specs = (
        P(None, "emit", "vx", "vy"),
        P(None, "emit", "vx", "vy"),
        P("vx", "vy"),
        P("vx", "vy"),
        P("vx", "vy"),
        P("emit", "vx", "vy", None),
        P("vx", "vy", None),
    )
    out_specs = (P("emit", "vx", "vy"), P("emit", "vx", "vy"))
    body = functools.partial(shards, mesh.shape["emit"], mesh.shape["vx"])
    return jax.shard_map(body, mesh=mesh, in_specs=in_specs, out_specs=out_specs, check_vma=False)
```

```python
import functools

import jax
import jax.numpy as jnp
from jax import lax
from jax.experimental import pallas as pl
from jax.experimental.pallas import tpu as pltpu
from jax.sharding import PartitionSpec as P

BR = 16
BC = 128
STEPS = 4
WIDE = 4
TOP = 16
HALO = 8
CHUNK = 32
ARRAYS = 9
MESH = pl.DeviceIdType.MESH


def lanes(count):
    return lax.broadcasted_iota(jnp.int32, (count, BC), 1)


def kernel(n_emit, n_vx, rows, fwd, adj, cour, dec, stren, listed_far, owner_far, grad, pres,
           *scratch):
    state = scratch[:ARRAYS]
    (saved, rowsend, rowrecv, colsend, colrecv, outgoing, incoming, listed, owner,
     load_sem, halo_send, halo_recv, block_send, block_recv, pres_sem, list_sem) = scratch[ARRAYS:]
    courant, decay, strength = state[6:]
    emit = lax.axis_index("emit")
    vx = lax.axis_index("vx")
    vy = lax.axis_index("vy")
    other = 1 - vy
    half = n_emit // 2
    parity = lax.rem(emit, 2)
    line = emit // 2
    partner = emit + 1 - 2 * parity
    per = incoming.shape[1]
    end = TOP + rows
    has_low = vx > 0
    has_high = vx < n_vx - 1

    sources = [fwd.at[at, 0] for at in range(3)] + [adj.at[at, 0] for at in range(3)] + [cour, dec, stren]
    loads = []
    for col in (other, vy):
        cut = pl.ds(pl.multiple_of(col * BC, BC), BC)
        for at in range(ARRAYS):
            copy = pltpu.make_async_copy(sources[at].at[:, cut], state[at].at[col, pl.ds(TOP, rows), :],
                                         load_sem.at[len(loads)])
            copy.start()
            loads.append(copy)

    barrier = pltpu.get_barrier_semaphore()

    def greet(where):
        pl.semaphore_signal(barrier, inc=1, device_id=where, device_id_type=MESH)

    greet((emit, vx, other))

    @pl.when(has_low)
    def _():
        greet((emit, vx - 1, vy))
        greet((emit, vx - 1, other))

    @pl.when(has_high)
    def _():
        greet((emit, vx + 1, vy))
        greet((emit, vx + 1, other))

    for step in range(1, n_emit):
        greet((lax.rem(emit + step, n_emit), vx, vy))

    lists = [pltpu.make_async_copy(listed_far, listed, list_sem.at[0]),
             pltpu.make_async_copy(owner_far, owner, list_sem.at[1])]
    for copy in lists:
        copy.start()

    @pl.when(vx == 0)
    def _():
        rowrecv[0] = jnp.zeros(rowrecv.shape[1:], jnp.float32)
        colrecv[pl.ds(0, HALO), :] = jnp.zeros((HALO, BC), jnp.float32)

    @pl.when(vx == n_vx - 1)
    def _():
        rowrecv[1] = jnp.zeros(rowrecv.shape[1:], jnp.float32)
        colrecv[pl.ds(HALO + rows, HALO), :] = jnp.zeros((HALO, BC), jnp.float32)

    for copy in loads[:ARRAYS]:
        copy.wait()
    base = other * (BC - WIDE)
    group = lax.rem(lanes(CHUNK) + (BC - base), BC) // WIDE

    def pack(at, carry):
        row = at * CHUNK
        packed = state[0][other, pl.ds(TOP + row, CHUNK), :]
        for which in range(1, ARRAYS):
            moved = pltpu.roll(state[which][other, pl.ds(TOP + row, CHUNK), :], WIDE * which, 1)
            packed = jnp.where(group == which, moved, packed)
        colsend[pl.ds(row, CHUNK), :] = packed
        return carry

    lax.fori_loop(0, rows // CHUNK, pack, 0)
    for copy in loads[ARRAYS:]:
        copy.wait()
    for which in range(ARRAYS):
        for col in range(2):
            place = pl.ds(WIDE * which, WIDE)
            rowsend[0, col, place, :] = state[which][col, pl.ds(TOP, WIDE), :]
            rowsend[1, col, place, :] = state[which][col, pl.ds(end - WIDE, WIDE), :]

    near = (vx > 0).astype(jnp.int32) + (vx < n_vx - 1).astype(jnp.int32)
    pl.semaphore_wait(barrier, n_emit + 2 * near)

    def remote(source, target, at, where):
        return pltpu.make_async_remote_copy(
            src_ref=source, dst_ref=target, send_sem=halo_send.at[at],
            recv_sem=halo_recv.at[at], device_id=where, device_id_type=MESH)

    side = remote(colsend, colrecv.at[pl.ds(HALO, rows), :], 2, (emit, vx, other))

    def to_high():
        return (remote(rowsend.at[1], rowrecv.at[0], 0, (emit, vx + 1, vy)),
                remote(colsend.at[pl.ds(rows - HALO, HALO), :], colrecv.at[pl.ds(0, HALO), :], 3,
                       (emit, vx + 1, other)))

    def to_low():
        return (remote(rowsend.at[0], rowrecv.at[1], 1, (emit, vx - 1, vy)),
                remote(colsend.at[pl.ds(0, HALO), :], colrecv.at[pl.ds(HALO + rows, HALO), :], 4,
                       (emit, vx - 1, other)))

    @pl.when(has_high)
    def _():
        for copy in to_high():
            copy.start()

    @pl.when(has_low)
    def _():
        for copy in to_low():
            copy.start()

    side.start()

    for copy in lists:
        copy.wait()
    bits = jnp.int32(0)
    for at in range(listed.shape[-1]):
        bits = bits | lax.shift_left(jnp.int32(1), listed[0, 0, 0, at])

    @pl.when(has_high)
    def _():
        for copy in to_low():
            copy.wait_recv()

    @pl.when(has_low)
    def _():
        for copy in to_high():
            copy.wait_recv()

    side.wait_recv()

    unpack_rows = (rows + 2 * HALO) // 2

    def unpack(at, carry):
        packed = colrecv[pl.ds(at * unpack_rows, unpack_rows), :]
        for which in range(ARRAYS):
            moved = packed if which == 0 else pltpu.roll(packed, BC - WIDE * which, 1)
            state[which][2, pl.ds(TOP - HALO + at * unpack_rows, unpack_rows), :] = moved
        return carry

    lax.fori_loop(0, 2, unpack, 0)
    for which in range(ARRAYS):
        for col in range(2):
            place = pl.ds(WIDE * which, WIDE)
            state[which][col, pl.ds(TOP - WIDE, WIDE), :] = rowrecv[0, col, place, :]
            state[which][col, pl.ds(end, WIDE), :] = rowrecv[1, col, place, :]

    east_on = (1 - vy).astype(jnp.float32)
    west_on = vy.astype(jnp.float32)

    def laplace_rows(field, row, count, cols):
        lane = lanes(count)
        center = [field[j, pl.ds(row, count), :] for j in range(3)]
        east = [pltpu.roll(center[j], BC - 1, 1) for j in range(3)]
        west = [pltpu.roll(center[j], 1, 1) for j in range(3)]
        curves = []
        for j in range(cols):
            after = east[(j + 1) % 3]
            before = west[(j + 2) % 3]
            if j == 1:
                after = after * east_on
            if j == 0:
                before = before * west_on
            right = jnp.where(lane == BC - 1, after, east[j])
            left = jnp.where(lane == 0, before, west[j])
            up = field[j, pl.ds(row - 1, count), :]
            down = field[j, pl.ds(row + 1, count), :]
            curves.append((up + down) + (left + right) - 4.0 * center[j])
        return center, curves

    def update(base, number, col, place, center, curve):
        memory = decay[col, place, :] * state[base + 2][col, place, :] + strength[col, place, :] * curve
        second = courant[col, place, :] * (curve - memory)
        following = (2.0 * center - state[base + (number + 1) % 2][col, place, :]) + second
        return memory, second, following

    def advance(base, number, row, count, cols):
        center, curves = laplace_rows(state[base + number % 2], row, count, cols)
        return [update(base, number, j, pl.ds(row, count), center[j], curves[j]) for j in range(cols)]

    def step_rows(number, row, count, keep):
        place = pl.ds(row, count)
        new = (number + 1) % 2
        results = []
        for base in (0, 3):
            result = advance(base, number, row, count, 3)
            for j in range(3):
                state[base + 2][j, place, :] = result[j][0]
                state[base + new][j, place, :] = result[j][2]
            results.append(result)
        if not keep:
            return
        forward, adjoint = results
        for j in range(2):
            if number < 3:
                saved[2 * number - 2, j, place, :] = forward[j][1]
                saved[2 * number - 1, j, place, :] = adjoint[j][2]
            else:
                saved[2, j, place, :] = (forward[j][1] * saved[3, j, place, :]
                                         + adjoint[j][2] * saved[2, j, place, :])

    for number in range(1, STEPS):
        def body(at, carry, number=number):
            step_rows(number, TOP + at * CHUNK, CHUNK, True)
            return carry

        lax.fori_loop(0, rows // CHUNK, body, 0)
        step_rows(number, TOP - HALO, HALO, False)
        step_rows(number, end, HALO, False)

    lane = lanes(BR)

    def block_step(base, block, row):
        field = state[base + STEPS % 2]
        col = block & 1
        before_col = jnp.where(col == 0, 2, 0)
        after_on = jnp.where(col == 1, east_on, 1.0)
        before_on = jnp.where(col == 0, west_on, 1.0)
        place = pl.ds(row, BR)
        center = field[col, place, :]
        after = pltpu.roll(field[col + 1, place, :], BC - 1, 1) * after_on
        before = pltpu.roll(field[before_col, place, :], 1, 1) * before_on
        right = jnp.where(lane == BC - 1, after, pltpu.roll(center, BC - 1, 1))
        left = jnp.where(lane == 0, before, pltpu.roll(center, 1, 1))
        up = field[col, pl.ds(row - 1, BR), :]
        down = field[col, pl.ds(row + 1, BR), :]
        curve = (up + down) + (left + right) - 4.0 * center
        return update(base, STEPS, col, place, center, curve)

    def masked(slot):
        block = owner[0, 0, slot]
        row = TOP + lax.shift_right_logical(block, 1) * BR
        col = block & 1
        hit = (lax.shift_right_logical(bits, block) & 1).astype(jnp.float32)
        _, second, _ = block_step(0, block, row)
        _, _, field = block_step(3, block, row)
        place = pl.ds(row, BR)
        total = (saved[2, col, place, :] + saved[0, col, place, :] * field
                 + saved[1, col, place, :] * second)
        return total * (hit * (1.0 / n_emit))

    def exchange(peer, slot):
        return pltpu.make_async_remote_copy(
            src_ref=outgoing.at[peer], dst_ref=incoming.at[slot], send_sem=block_send.at[peer],
            recv_sem=block_recv.at[slot], device_id=(peer, vx, vy), device_id_type=MESH)

    offsets = [half // 2 + at for at in range(half - half // 2)] + list(range(1, half // 2))
    peers = [2 * lax.rem(line + offset, half) + side_of for offset in offsets
             for side_of in (parity, 1 - parity)] + [partner]
    for peer in peers:
        parts = [masked(peer * per + slot) for slot in range(per)]
        for slot in range(per):
            outgoing[peer, slot] = parts[slot]
        exchange(peer, emit).start()
    parts = [masked(emit * per + slot) for slot in range(per)]
    for slot in range(per):
        incoming[emit, slot] = parts[slot]

    def last_body(at, carry):
        row = TOP + at * CHUNK
        forward = advance(0, STEPS, row, CHUNK, 2)
        for j in range(2):
            state[(STEPS + 1) % 2][j, pl.ds(row, CHUNK), :] = forward[j][2]
        return carry

    lax.fori_loop(0, rows // CHUNK, last_body, 0)

    pres_copies = []
    for j in range(2):
        copy = pltpu.make_async_copy(state[(STEPS + 1) % 2].at[j, pl.ds(TOP, rows), :],
                                     pres.at[0, :, pl.ds(j * BC, BC)], pres_sem.at[j])
        copy.start()
        pres_copies.append(copy)

    side.wait_send()

    @pl.when(has_high)
    def _():
        for copy in to_high():
            copy.wait_send()

    @pl.when(has_low)
    def _():
        for copy in to_low():
            copy.wait_send()

    for peer in peers[::-1]:
        exchange(peer, peer).wait()
    total = incoming[0]
    for at in range(1, n_emit):
        total = total + incoming[at]
    grad[...] = total
    for copy in pres_copies:
        copy.wait()


def hand_over(found, waves, grad, pres, found_here, waves_here, sem):
    parts = 4
    rows = waves.shape[1] // parts
    steps = [(found, found_here, grad)]
    for at in range(parts):
        place = pl.ds(at * rows, rows)
        steps.append((waves.at[:, place, :], waves_here.at[:, place, :], pres.at[:, place, :]))
    taken = [pltpu.make_async_copy(source, here, sem.at[0, at]) for at, (source, here, _) in enumerate(steps)]
    given = [pltpu.make_async_copy(here, target, sem.at[1, at]) for at, (_, here, target) in enumerate(steps)]
    for copy in taken:
        copy.start()
    for into, out in zip(taken, given):
        into.wait()
        out.start()
    for copy in given:
        copy.wait()


def shards(n_emit, n_vx, fwd_state, adj_state, courant, decay_rate, strength, footprint, owner_map):
    rows = fwd_state.shape[2]
    blocks = owner_map.shape[-1]
    per = blocks // n_emit
    padded = rows + 2 * TOP
    anywhere = pl.BlockSpec(memory_space=pl.ANY)
    far = pl.BlockSpec(memory_space=pltpu.HBM)

    def blocks_of(count):
        return pltpu.VMEM((count, per, BR, BC), jnp.float32)

    found, waves = pl.pallas_call(
        functools.partial(kernel, n_emit, n_vx, rows),
        out_shape=(jax.ShapeDtypeStruct((per, BR, BC), jnp.float32),
                   jax.ShapeDtypeStruct((1, rows, 2 * BC), jnp.float32)),
        in_specs=[far] * 7,
        out_specs=(pl.BlockSpec(memory_space=pltpu.VMEM), anywhere),
        scratch_shapes=[pltpu.VMEM((3, padded, BC), jnp.float32)] * ARRAYS + [
            pltpu.VMEM((4, 2, padded, BC), jnp.float32),
            pltpu.VMEM((2, 2, 40, BC), jnp.float32),
            pltpu.VMEM((2, 2, 40, BC), jnp.float32),
            pltpu.VMEM((rows, BC), jnp.float32),
            pltpu.VMEM((rows + 2 * HALO, BC), jnp.float32),
        ] + [blocks_of(n_emit)] * 2 + [
            pltpu.SMEM(footprint.shape, jnp.int32),
            pltpu.SMEM(owner_map.shape, jnp.int32),
            pltpu.SemaphoreType.DMA((2 * ARRAYS,)),
            pltpu.SemaphoreType.DMA((5,)),
            pltpu.SemaphoreType.DMA((5,)),
            pltpu.SemaphoreType.DMA((n_emit,)),
            pltpu.SemaphoreType.DMA((n_emit,)),
            pltpu.SemaphoreType.DMA((2,)),
            pltpu.SemaphoreType.DMA((2,)),
        ],
        compiler_params=pltpu.CompilerParams(collective_id=0, has_side_effects=True),
        name="waves",
    )(fwd_state, adj_state, courant, decay_rate, strength, footprint, owner_map)
    return pl.pallas_call(
        hand_over,
        out_shape=(jax.ShapeDtypeStruct(found.shape, jnp.float32),
                   jax.ShapeDtypeStruct(waves.shape, jnp.float32)),
        in_specs=[anywhere] * 2,
        out_specs=(anywhere, anywhere),
        scratch_shapes=[pltpu.VMEM(found.shape, jnp.float32), pltpu.VMEM(waves.shape, jnp.float32),
                        pltpu.SemaphoreType.DMA((2, 5))],
        name="hand_over",
    )(found, waves)


def solution(mesh):
    in_specs = (
        P(None, "emit", "vx", "vy"),
        P(None, "emit", "vx", "vy"),
        P("vx", "vy"),
        P("vx", "vy"),
        P("vx", "vy"),
        P("emit", "vx", "vy", None),
        P("vx", "vy", None),
    )
    out_specs = (P("emit", "vx", "vy"), P("emit", "vx", "vy"))
    body = functools.partial(shards, mesh.shape["emit"], mesh.shape["vx"])
    return jax.shard_map(body, mesh=mesh, in_specs=in_specs, out_specs=out_specs, check_vma=False)
```

```python
import functools

import jax
import jax.numpy as jnp
from jax import lax
from jax.experimental import pallas as pl
from jax.experimental.pallas import tpu as pltpu
from jax.sharding import PartitionSpec as P

BR = 16
BC = 128
STEPS = 4
WIDE = 4
TOP = 16
HALO = 8
CHUNK = 32
ARRAYS = 9
MESH = pl.DeviceIdType.MESH


def lanes(count):
    return lax.broadcasted_iota(jnp.int32, (count, BC), 1)


def kernel(n_emit, n_vx, rows, fwd, adj, cour, dec, stren, listed_far, owner_far, grad, pres,
           *scratch):
    state = scratch[:ARRAYS]
    (saved, rowsend, rowrecv, colsend, colrecv, outgoing, incoming, first_out, first_in, own_part, second_out, second_in,
     listed, owner, load_sem, halo_send, halo_recv, block_send, block_recv, first_send, first_recv,
     second_send, second_recv, pres_sem, list_sem) = scratch[ARRAYS:]
    courant, decay, strength = state[6:]
    emit = lax.axis_index("emit")
    vx = lax.axis_index("vx")
    vy = lax.axis_index("vy")
    other = 1 - vy
    half = n_emit // 2
    parity = lax.rem(emit, 2)
    line = emit // 2
    partner = emit + 1 - 2 * parity
    joint = second_in.shape[1]
    per = grad.shape[0]
    end = TOP + rows
    has_low = vx > 0
    has_high = vx < n_vx - 1

    sources = [fwd.at[at, 0] for at in range(3)] + [adj.at[at, 0] for at in range(3)] + [cour, dec, stren]
    loads = []
    for col in (other, vy):
        cut = pl.ds(pl.multiple_of(col * BC, BC), BC)
        for at in range(ARRAYS):
            copy = pltpu.make_async_copy(sources[at].at[:, cut], state[at].at[col, pl.ds(TOP, rows), :],
                                         load_sem.at[len(loads)])
            copy.start()
            loads.append(copy)

    barrier = pltpu.get_barrier_semaphore()

    def greet(where):
        pl.semaphore_signal(barrier, inc=1, device_id=where, device_id_type=MESH)

    greet((emit, vx, other))

    @pl.when(has_low)
    def _():
        greet((emit, vx - 1, vy))
        greet((emit, vx - 1, other))

    @pl.when(has_high)
    def _():
        greet((emit, vx + 1, vy))
        greet((emit, vx + 1, other))

    for step in range(1, n_emit):
        greet((lax.rem(emit + step, n_emit), vx, vy))

    lists = [pltpu.make_async_copy(listed_far, listed, list_sem.at[0]),
             pltpu.make_async_copy(owner_far, owner, list_sem.at[1])]
    for copy in lists:
        copy.start()

    @pl.when(vx == 0)
    def _():
        rowrecv[0] = jnp.zeros(rowrecv.shape[1:], jnp.float32)
        colrecv[pl.ds(0, HALO), :] = jnp.zeros((HALO, BC), jnp.float32)

    @pl.when(vx == n_vx - 1)
    def _():
        rowrecv[1] = jnp.zeros(rowrecv.shape[1:], jnp.float32)
        colrecv[pl.ds(HALO + rows, HALO), :] = jnp.zeros((HALO, BC), jnp.float32)

    for copy in loads[:ARRAYS]:
        copy.wait()
    base = other * (BC - WIDE)
    group = lax.rem(lanes(CHUNK) + (BC - base), BC) // WIDE

    def pack(at, carry):
        row = at * CHUNK
        packed = state[0][other, pl.ds(TOP + row, CHUNK), :]
        for which in range(1, ARRAYS):
            moved = pltpu.roll(state[which][other, pl.ds(TOP + row, CHUNK), :], WIDE * which, 1)
            packed = jnp.where(group == which, moved, packed)
        colsend[pl.ds(row, CHUNK), :] = packed
        return carry

    lax.fori_loop(0, rows // CHUNK, pack, 0)
    near = (vx > 0).astype(jnp.int32) + (vx < n_vx - 1).astype(jnp.int32)
    pl.semaphore_wait(barrier, n_emit + 2 * near)

    def remote(source, target, at, where):
        return pltpu.make_async_remote_copy(
            src_ref=source, dst_ref=target, send_sem=halo_send.at[at],
            recv_sem=halo_recv.at[at], device_id=where, device_id_type=MESH)

    side = remote(colsend, colrecv.at[pl.ds(HALO, rows), :], 2, (emit, vx, other))

    side.start()

    for copy in loads[ARRAYS:]:
        copy.wait()
    for which in range(ARRAYS):
        for col in range(2):
            place = pl.ds(WIDE * which, WIDE)
            rowsend[0, col, place, :] = state[which][col, pl.ds(TOP, WIDE), :]
            rowsend[1, col, place, :] = state[which][col, pl.ds(end - WIDE, WIDE), :]

    def to_high():
        return (remote(rowsend.at[1], rowrecv.at[0], 0, (emit, vx + 1, vy)),
                remote(colsend.at[pl.ds(rows - HALO, HALO), :], colrecv.at[pl.ds(0, HALO), :], 3,
                       (emit, vx + 1, other)))

    def to_low():
        return (remote(rowsend.at[0], rowrecv.at[1], 1, (emit, vx - 1, vy)),
                remote(colsend.at[pl.ds(0, HALO), :], colrecv.at[pl.ds(HALO + rows, HALO), :], 4,
                       (emit, vx - 1, other)))

    @pl.when(has_high)
    def _():
        for copy in to_high():
            copy.start()

    @pl.when(has_low)
    def _():
        for copy in to_low():
            copy.start()

    for copy in lists:
        copy.wait()
    bits = jnp.int32(0)
    for at in range(listed.shape[-1]):
        bits = bits | lax.shift_left(jnp.int32(1), listed[0, 0, 0, at])

    @pl.when(has_high)
    def _():
        for copy in to_low():
            copy.wait_recv()

    @pl.when(has_low)
    def _():
        for copy in to_high():
            copy.wait_recv()

    side.wait_recv()

    unpack_rows = (rows + 2 * HALO) // 2

    def unpack(at, carry):
        packed = colrecv[pl.ds(at * unpack_rows, unpack_rows), :]
        for which in range(ARRAYS):
            moved = packed if which == 0 else pltpu.roll(packed, BC - WIDE * which, 1)
            state[which][2, pl.ds(TOP - HALO + at * unpack_rows, unpack_rows), :] = moved
        return carry

    lax.fori_loop(0, 2, unpack, 0)
    for which in range(ARRAYS):
        for col in range(2):
            place = pl.ds(WIDE * which, WIDE)
            state[which][col, pl.ds(TOP - WIDE, WIDE), :] = rowrecv[0, col, place, :]
            state[which][col, pl.ds(end, WIDE), :] = rowrecv[1, col, place, :]

    east_on = (1 - vy).astype(jnp.float32)
    west_on = vy.astype(jnp.float32)

    def laplace_rows(field, row, count, cols):
        lane = lanes(count)
        center = [field[j, pl.ds(row, count), :] for j in range(3)]
        east = [pltpu.roll(center[j], BC - 1, 1) for j in range(3)]
        west = [pltpu.roll(center[j], 1, 1) for j in range(3)]
        curves = []
        for j in range(cols):
            after = east[(j + 1) % 3]
            before = west[(j + 2) % 3]
            if j == 1:
                after = after * east_on
            if j == 0:
                before = before * west_on
            right = jnp.where(lane == BC - 1, after, east[j])
            left = jnp.where(lane == 0, before, west[j])
            up = field[j, pl.ds(row - 1, count), :]
            down = field[j, pl.ds(row + 1, count), :]
            curves.append((up + down) + (left + right) - 4.0 * center[j])
        return center, curves

    def update(base, number, col, place, center, curve):
        memory = decay[col, place, :] * state[base + 2][col, place, :] + strength[col, place, :] * curve
        second = courant[col, place, :] * (curve - memory)
        following = (2.0 * center - state[base + (number + 1) % 2][col, place, :]) + second
        return memory, second, following

    def advance(base, number, row, count, cols):
        center, curves = laplace_rows(state[base + number % 2], row, count, cols)
        return [update(base, number, j, pl.ds(row, count), center[j], curves[j]) for j in range(cols)]

    def step_rows(number, row, count, keep):
        place = pl.ds(row, count)
        new = (number + 1) % 2
        results = []
        for base in (0, 3):
            result = advance(base, number, row, count, 3)
            for j in range(3):
                state[base + 2][j, place, :] = result[j][0]
                state[base + new][j, place, :] = result[j][2]
            results.append(result)
        if not keep:
            return
        forward, adjoint = results
        for j in range(2):
            if number < 3:
                saved[2 * number - 2, j, place, :] = forward[j][1]
                saved[2 * number - 1, j, place, :] = adjoint[j][2]
            else:
                saved[2, j, place, :] = (forward[j][1] * saved[3, j, place, :]
                                         + adjoint[j][2] * saved[2, j, place, :])

    for number in range(1, STEPS):
        def body(at, carry, number=number):
            step_rows(number, TOP + at * CHUNK, CHUNK, True)
            return carry

        lax.fori_loop(0, rows // CHUNK, body, 0)
        step_rows(number, TOP - HALO, HALO, False)
        step_rows(number, end, HALO, False)

    lane = lanes(BR)

    def block_step(base, block, row):
        field = state[base + STEPS % 2]
        col = block & 1
        before_col = jnp.where(col == 0, 2, 0)
        after_on = jnp.where(col == 1, east_on, 1.0)
        before_on = jnp.where(col == 0, west_on, 1.0)
        place = pl.ds(row, BR)
        center = field[col, place, :]
        after = pltpu.roll(field[col + 1, place, :], BC - 1, 1) * after_on
        before = pltpu.roll(field[before_col, place, :], 1, 1) * before_on
        right = jnp.where(lane == BC - 1, after, pltpu.roll(center, BC - 1, 1))
        left = jnp.where(lane == 0, before, pltpu.roll(center, 1, 1))
        up = field[col, pl.ds(row - 1, BR), :]
        down = field[col, pl.ds(row + 1, BR), :]
        curve = (up + down) + (left + right) - 4.0 * center
        return update(base, STEPS, col, place, center, curve)

    def masked(slot):
        block = owner[0, 0, slot]
        row = TOP + lax.shift_right_logical(block, 1) * BR
        col = block & 1
        hit = (lax.shift_right_logical(bits, block) & 1).astype(jnp.float32)
        _, second, _ = block_step(0, block, row)
        _, _, field = block_step(3, block, row)
        place = pl.ds(row, BR)
        total = (saved[2, col, place, :] + saved[0, col, place, :] * field
                 + saved[1, col, place, :] * second)
        return total * (hit * (1.0 / n_emit))

    def exchange(peer, slot):
        return pltpu.make_async_remote_copy(
            src_ref=outgoing.at[peer], dst_ref=incoming.at[slot], send_sem=block_send.at[peer],
            recv_sem=block_recv.at[slot], device_id=(peer, vx, vy), device_id_type=MESH)

    def to_partner(at):
        return pltpu.make_async_remote_copy(
            src_ref=first_out.at[at], dst_ref=first_in.at[at], send_sem=first_send.at[at],
            recv_sem=first_recv.at[at], device_id=(partner, vx, vy), device_id_type=MESH)

    def to_owner(at, slot):
        return pltpu.make_async_remote_copy(
            src_ref=second_out.at[at], dst_ref=second_in.at[slot], send_sem=second_send.at[at],
            recv_sem=second_recv.at[slot], device_id=(2 * at + parity, vx, vy), device_id_type=MESH)

    def fill(target, at, peer, slots):
        parts = [masked(peer * per + slot) for slot in slots]
        for which, part in enumerate(parts):
            target[at, which] = part

    offsets = [half // 2 + at for at in range(half - half // 2)] + list(range(1, half // 2))
    order = [lax.rem(line + offset, half) for offset in offsets] + [line]
    peers = [2 * at + side_of for at in order[:-1] for side_of in (parity, 1 - parity)] + [partner]
    early, late = range(joint), range(joint, per)

    for at in order:
        fill(first_out, at, 2 * at + 1 - parity, early)
        to_partner(at).start()
        if joint < per and at is not line:
            fill(outgoing, 2 * at + parity, 2 * at + parity, late)
            exchange(2 * at + parity, emit).start()
    if joint < per:
        for peer in peers[1::2] + [partner]:
            fill(outgoing, peer, peer, late)
            exchange(peer, emit).start()
    for at in order:
        fill(own_part, at, 2 * at + parity, early)
    for at in order[:-1]:
        to_partner(at).wait_recv()
        second_out[at] = own_part[at] + first_in[at]
        to_owner(at, line).start()
    to_partner(line).wait_recv()
    second_in[line] = own_part[line] + first_in[line]
    if joint < per:
        fill(incoming, emit, emit, late)

    def last_body(at, carry):
        row = TOP + at * CHUNK
        forward = advance(0, STEPS, row, CHUNK, 2)
        for j in range(2):
            state[(STEPS + 1) % 2][j, pl.ds(row, CHUNK), :] = forward[j][2]
        return carry

    lax.fori_loop(0, rows // CHUNK, last_body, 0)

    pres_copies = []
    for j in range(2):
        copy = pltpu.make_async_copy(state[(STEPS + 1) % 2].at[j, pl.ds(TOP, rows), :],
                                     pres.at[0, :, pl.ds(j * BC, BC)], pres_sem.at[j])
        copy.start()
        pres_copies.append(copy)

    side.wait_send()

    @pl.when(has_high)
    def _():
        for copy in to_high():
            copy.wait_send()

    @pl.when(has_low)
    def _():
        for copy in to_low():
            copy.wait_send()

    for at in range(half):
        to_partner(at).wait_send()
    if joint < per:
        for peer in peers[::-1]:
            exchange(peer, peer).wait()
        total = incoming[0]
        for at in range(1, n_emit):
            total = total + incoming[at]
        grad[pl.ds(joint, per - joint)] = total
    for at in order[:-1]:
        to_owner(at, at).wait()
    total = second_in[0]
    for at in range(1, half):
        total = total + second_in[at]
    grad[pl.ds(0, joint)] = total
    for copy in pres_copies:
        copy.wait()


def hand_over(found, waves, grad, pres, found_here, waves_here, sem):
    parts = 4
    rows = waves.shape[1] // parts
    steps = [(found, found_here, grad)]
    for at in range(parts):
        place = pl.ds(at * rows, rows)
        steps.append((waves.at[:, place, :], waves_here.at[:, place, :], pres.at[:, place, :]))
    taken = [pltpu.make_async_copy(source, here, sem.at[0, at]) for at, (source, here, _) in enumerate(steps)]
    given = [pltpu.make_async_copy(here, target, sem.at[1, at]) for at, (_, here, target) in enumerate(steps)]
    for copy in taken:
        copy.start()
    for into, out in zip(taken, given):
        into.wait()
        out.start()
    for copy in given:
        copy.wait()


def shards(n_emit, n_vx, fwd_state, adj_state, courant, decay_rate, strength, footprint, owner_map):
    rows = fwd_state.shape[2]
    blocks = owner_map.shape[-1]
    per = blocks // n_emit
    half = n_emit // 2
    joint = max(1, per // 2)
    direct = max(1, per - joint)
    padded = rows + 2 * TOP
    anywhere = pl.BlockSpec(memory_space=pl.ANY)
    far = pl.BlockSpec(memory_space=pltpu.HBM)

    def blocks_of(count, slots):
        return pltpu.VMEM((count, slots, BR, BC), jnp.float32)

    found, waves = pl.pallas_call(
        functools.partial(kernel, n_emit, n_vx, rows),
        out_shape=(jax.ShapeDtypeStruct((per, BR, BC), jnp.float32),
                   jax.ShapeDtypeStruct((1, rows, 2 * BC), jnp.float32)),
        in_specs=[far] * 7,
        out_specs=(pl.BlockSpec(memory_space=pltpu.VMEM), anywhere),
        scratch_shapes=[pltpu.VMEM((3, padded, BC), jnp.float32)] * ARRAYS + [
            pltpu.VMEM((4, 2, padded, BC), jnp.float32),
            pltpu.VMEM((2, 2, 40, BC), jnp.float32),
            pltpu.VMEM((2, 2, 40, BC), jnp.float32),
            pltpu.VMEM((rows, BC), jnp.float32),
            pltpu.VMEM((rows + 2 * HALO, BC), jnp.float32),
        ] + [blocks_of(n_emit, direct)] * 2 + [blocks_of(half, joint)] * 5 + [
            pltpu.SMEM(footprint.shape, jnp.int32),
            pltpu.SMEM(owner_map.shape, jnp.int32),
            pltpu.SemaphoreType.DMA((2 * ARRAYS,)),
            pltpu.SemaphoreType.DMA((5,)),
            pltpu.SemaphoreType.DMA((5,)),
            pltpu.SemaphoreType.DMA((n_emit,)),
            pltpu.SemaphoreType.DMA((n_emit,)),
            pltpu.SemaphoreType.DMA((half,)),
            pltpu.SemaphoreType.DMA((half,)),
            pltpu.SemaphoreType.DMA((half,)),
            pltpu.SemaphoreType.DMA((half,)),
            pltpu.SemaphoreType.DMA((2,)),
            pltpu.SemaphoreType.DMA((2,)),
        ],
        compiler_params=pltpu.CompilerParams(collective_id=0, has_side_effects=True),
        name="waves",
    )(fwd_state, adj_state, courant, decay_rate, strength, footprint, owner_map)
    return pl.pallas_call(
        hand_over,
        out_shape=(jax.ShapeDtypeStruct(found.shape, jnp.float32),
                   jax.ShapeDtypeStruct(waves.shape, jnp.float32)),
        in_specs=[anywhere] * 2,
        out_specs=(anywhere, anywhere),
        scratch_shapes=[pltpu.VMEM(found.shape, jnp.float32), pltpu.VMEM(waves.shape, jnp.float32),
                        pltpu.SemaphoreType.DMA((2, 5))],
        name="hand_over",
    )(found, waves)


def solution(mesh):
    in_specs = (
        P(None, "emit", "vx", "vy"),
        P(None, "emit", "vx", "vy"),
        P("vx", "vy"),
        P("vx", "vy"),
        P("vx", "vy"),
        P("emit", "vx", "vy", None),
        P("vx", "vy", None),
    )
    out_specs = (P("emit", "vx", "vy"), P("emit", "vx", "vy"))
    body = functools.partial(shards, mesh.shape["emit"], mesh.shape["vx"])
    return jax.shard_map(body, mesh=mesh, in_specs=in_specs, out_specs=out_specs, check_vma=False)
```

```python
import functools

import jax
import jax.numpy as jnp
from jax import lax
from jax.experimental import pallas as pl
from jax.experimental.pallas import tpu as pltpu
from jax.sharding import PartitionSpec as P

BR = 16
BC = 128
STEPS = 4
WIDE = 4
TOP = 16
HALO = 8
CHUNK = 32
ARRAYS = 9
MESH = pl.DeviceIdType.MESH


def lanes(count):
    return lax.broadcasted_iota(jnp.int32, (count, BC), 1)


def kernel(n_emit, n_vx, rows, fwd, adj, cour, dec, stren, listed_far, owner_far, grad, pres,
           *scratch):
    state = scratch[:ARRAYS]
    (saved, rowsend, rowrecv, colsend, colrecv, outgoing, incoming, listed, owner,
     load_sem, halo_send, halo_recv, block_send, block_recv, pres_sem, list_sem) = scratch[ARRAYS:]
    courant, decay, strength = state[6:]
    emit = lax.axis_index("emit")
    vx = lax.axis_index("vx")
    vy = lax.axis_index("vy")
    other = 1 - vy
    half = n_emit // 2
    parity = lax.rem(emit, 2)
    line = emit // 2
    partner = emit + 1 - 2 * parity
    per = incoming.shape[1]
    end = TOP + rows
    has_low = vx > 0
    has_high = vx < n_vx - 1

    sources = [fwd.at[at, 0] for at in range(3)] + [adj.at[at, 0] for at in range(3)] + [cour, dec, stren]
    loads = []
    for col in (other, vy):
        cut = pl.ds(pl.multiple_of(col * BC, BC), BC)
        for at in range(ARRAYS):
            copy = pltpu.make_async_copy(sources[at].at[:, cut], state[at].at[col, pl.ds(TOP, rows), :],
                                         load_sem.at[len(loads)])
            copy.start()
            loads.append(copy)

    barrier = pltpu.get_barrier_semaphore()

    def greet(where):
        pl.semaphore_signal(barrier, inc=1, device_id=where, device_id_type=MESH)

    greet((emit, vx, other))

    @pl.when(has_low)
    def _():
        greet((emit, vx - 1, vy))
        greet((emit, vx - 1, other))

    @pl.when(has_high)
    def _():
        greet((emit, vx + 1, vy))
        greet((emit, vx + 1, other))

    for step in range(1, n_emit):
        greet((lax.rem(emit + step, n_emit), vx, vy))

    lists = [pltpu.make_async_copy(listed_far, listed, list_sem.at[0]),
             pltpu.make_async_copy(owner_far, owner, list_sem.at[1])]
    for copy in lists:
        copy.start()

    @pl.when(vx == 0)
    def _():
        rowrecv[0] = jnp.zeros(rowrecv.shape[1:], jnp.float32)
        colrecv[pl.ds(0, HALO), :] = jnp.zeros((HALO, BC), jnp.float32)

    @pl.when(vx == n_vx - 1)
    def _():
        rowrecv[1] = jnp.zeros(rowrecv.shape[1:], jnp.float32)
        colrecv[pl.ds(HALO + rows, HALO), :] = jnp.zeros((HALO, BC), jnp.float32)

    for copy in loads[:ARRAYS]:
        copy.wait()
    base = other * (BC - WIDE)
    group = lax.rem(lanes(CHUNK) + (BC - base), BC) // WIDE

    def pack(at, carry):
        row = at * CHUNK
        packed = state[0][other, pl.ds(TOP + row, CHUNK), :]
        for which in range(1, ARRAYS):
            moved = pltpu.roll(state[which][other, pl.ds(TOP + row, CHUNK), :], WIDE * which, 1)
            packed = jnp.where(group == which, moved, packed)
        colsend[pl.ds(row, CHUNK), :] = packed
        return carry

    lax.fori_loop(0, rows // CHUNK, pack, 0)
    near = (vx > 0).astype(jnp.int32) + (vx < n_vx - 1).astype(jnp.int32)
    pl.semaphore_wait(barrier, n_emit + 2 * near)

    def remote(source, target, at, where):
        return pltpu.make_async_remote_copy(
            src_ref=source, dst_ref=target, send_sem=halo_send.at[at],
            recv_sem=halo_recv.at[at], device_id=where, device_id_type=MESH)

    side = remote(colsend, colrecv.at[pl.ds(HALO, rows), :], 2, (emit, vx, other))

    side.start()

    for copy in loads[ARRAYS:]:
        copy.wait()
    for which in range(ARRAYS):
        for col in range(2):
            place = pl.ds(WIDE * which, WIDE)
            rowsend[0, col, place, :] = state[which][col, pl.ds(TOP, WIDE), :]
            rowsend[1, col, place, :] = state[which][col, pl.ds(end - WIDE, WIDE), :]

    def to_high():
        return (remote(rowsend.at[1], rowrecv.at[0], 0, (emit, vx + 1, vy)),
                remote(colsend.at[pl.ds(rows - HALO, HALO), :], colrecv.at[pl.ds(0, HALO), :], 3,
                       (emit, vx + 1, other)))

    def to_low():
        return (remote(rowsend.at[0], rowrecv.at[1], 1, (emit, vx - 1, vy)),
                remote(colsend.at[pl.ds(0, HALO), :], colrecv.at[pl.ds(HALO + rows, HALO), :], 4,
                       (emit, vx - 1, other)))

    @pl.when(has_high)
    def _():
        for copy in to_high():
            copy.start()

    @pl.when(has_low)
    def _():
        for copy in to_low():
            copy.start()

    for copy in lists:
        copy.wait()
    bits = jnp.int32(0)
    for at in range(listed.shape[-1]):
        bits = bits | lax.shift_left(jnp.int32(1), listed[0, 0, 0, at])

    @pl.when(has_high)
    def _():
        for copy in to_low():
            copy.wait_recv()

    @pl.when(has_low)
    def _():
        for copy in to_high():
            copy.wait_recv()

    side.wait_recv()

    unpack_rows = (rows + 2 * HALO) // 2

    def unpack(at, carry):
        packed = colrecv[pl.ds(at * unpack_rows, unpack_rows), :]
        for which in range(ARRAYS):
            moved = packed if which == 0 else pltpu.roll(packed, BC - WIDE * which, 1)
            state[which][2, pl.ds(TOP - HALO + at * unpack_rows, unpack_rows), :] = moved
        return carry

    lax.fori_loop(0, 2, unpack, 0)
    for which in range(ARRAYS):
        for col in range(2):
            place = pl.ds(WIDE * which, WIDE)
            state[which][col, pl.ds(TOP - WIDE, WIDE), :] = rowrecv[0, col, place, :]
            state[which][col, pl.ds(end, WIDE), :] = rowrecv[1, col, place, :]

    east_on = (1 - vy).astype(jnp.float32)
    west_on = vy.astype(jnp.float32)

    def laplace_rows(field, row, count, cols):
        lane = lanes(count)
        center = [field[j, pl.ds(row, count), :] for j in range(3)]
        east = [pltpu.roll(center[j], BC - 1, 1) for j in range(3)]
        west = [pltpu.roll(center[j], 1, 1) for j in range(3)]
        curves = []
        for j in range(cols):
            after = east[(j + 1) % 3]
            before = west[(j + 2) % 3]
            if j == 1:
                after = after * east_on
            if j == 0:
                before = before * west_on
            right = jnp.where(lane == BC - 1, after, east[j])
            left = jnp.where(lane == 0, before, west[j])
            up = field[j, pl.ds(row - 1, count), :]
            down = field[j, pl.ds(row + 1, count), :]
            curves.append((up + down) + (left + right) - 4.0 * center[j])
        return center, curves

    def update(base, number, col, place, center, curve):
        memory = decay[col, place, :] * state[base + 2][col, place, :] + strength[col, place, :] * curve
        second = courant[col, place, :] * (curve - memory)
        following = (2.0 * center - state[base + (number + 1) % 2][col, place, :]) + second
        return memory, second, following

    def advance(base, number, row, count, cols):
        center, curves = laplace_rows(state[base + number % 2], row, count, cols)
        return [update(base, number, j, pl.ds(row, count), center[j], curves[j]) for j in range(cols)]

    def step_rows(number, row, count, keep):
        place = pl.ds(row, count)
        new = (number + 1) % 2
        results = []
        for base in (0, 3):
            result = advance(base, number, row, count, 3)
            for j in range(3):
                state[base + 2][j, place, :] = result[j][0]
                state[base + new][j, place, :] = result[j][2]
            results.append(result)
        if not keep:
            return
        forward, adjoint = results
        for j in range(2):
            if number < 3:
                saved[2 * number - 2, j, place, :] = forward[j][1]
                saved[2 * number - 1, j, place, :] = adjoint[j][2]
            else:
                saved[2, j, place, :] = (forward[j][1] * saved[3, j, place, :]
                                         + adjoint[j][2] * saved[2, j, place, :])

    for number in range(1, STEPS):
        def body(at, carry, number=number):
            step_rows(number, TOP + at * CHUNK, CHUNK, True)
            return carry

        lax.fori_loop(0, rows // CHUNK, body, 0)
        step_rows(number, TOP - HALO, HALO, False)
        step_rows(number, end, HALO, False)

    lane = lanes(BR)

    def block_step(base, block, row):
        field = state[base + STEPS % 2]
        col = block & 1
        before_col = jnp.where(col == 0, 2, 0)
        after_on = jnp.where(col == 1, east_on, 1.0)
        before_on = jnp.where(col == 0, west_on, 1.0)
        place = pl.ds(row, BR)
        center = field[col, place, :]
        after = pltpu.roll(field[col + 1, place, :], BC - 1, 1) * after_on
        before = pltpu.roll(field[before_col, place, :], 1, 1) * before_on
        right = jnp.where(lane == BC - 1, after, pltpu.roll(center, BC - 1, 1))
        left = jnp.where(lane == 0, before, pltpu.roll(center, 1, 1))
        up = field[col, pl.ds(row - 1, BR), :]
        down = field[col, pl.ds(row + 1, BR), :]
        curve = (up + down) + (left + right) - 4.0 * center
        return update(base, STEPS, col, place, center, curve)

    def masked(slot):
        block = owner[0, 0, slot]
        row = TOP + lax.shift_right_logical(block, 1) * BR
        col = block & 1
        hit = (lax.shift_right_logical(bits, block) & 1).astype(jnp.float32)
        _, second, _ = block_step(0, block, row)
        _, _, field = block_step(3, block, row)
        place = pl.ds(row, BR)
        total = (saved[2, col, place, :] + saved[0, col, place, :] * field
                 + saved[1, col, place, :] * second)
        return total * (hit * (1.0 / n_emit))

    def exchange(peer, slot):
        return pltpu.make_async_remote_copy(
            src_ref=outgoing.at[peer], dst_ref=incoming.at[slot], send_sem=block_send.at[peer],
            recv_sem=block_recv.at[slot], device_id=(peer, vx, vy), device_id_type=MESH)

    offsets = [half // 2 + at for at in range(half - half // 2)] + list(range(1, half // 2))
    peers = [2 * lax.rem(line + offset, half) + side_of for offset in offsets
             for side_of in (parity, 1 - parity)] + [partner]
    for peer in peers:
        parts = [masked(peer * per + slot) for slot in range(per)]
        for slot in range(per):
            outgoing[peer, slot] = parts[slot]
        exchange(peer, emit).start()
    parts = [masked(emit * per + slot) for slot in range(per)]
    for slot in range(per):
        incoming[emit, slot] = parts[slot]

    def last_body(at, carry):
        row = TOP + at * CHUNK
        forward = advance(0, STEPS, row, CHUNK, 2)
        for j in range(2):
            state[(STEPS + 1) % 2][j, pl.ds(row, CHUNK), :] = forward[j][2]
        return carry

    lax.fori_loop(0, rows // CHUNK, last_body, 0)

    pres_copies = []
    for j in range(2):
        copy = pltpu.make_async_copy(state[(STEPS + 1) % 2].at[j, pl.ds(TOP, rows), :],
                                     pres.at[0, :, pl.ds(j * BC, BC)], pres_sem.at[j])
        copy.start()
        pres_copies.append(copy)

    side.wait_send()

    @pl.when(has_high)
    def _():
        for copy in to_high():
            copy.wait_send()

    @pl.when(has_low)
    def _():
        for copy in to_low():
            copy.wait_send()

    for peer in peers[::-1]:
        exchange(peer, peer).wait()
    total = incoming[0]
    for at in range(1, n_emit):
        total = total + incoming[at]
    grad[...] = total
    for copy in pres_copies:
        copy.wait()


def hand_over(found, waves, grad, pres, found_here, waves_here, sem):
    parts = 4
    rows = waves.shape[1] // parts
    steps = [(found, found_here, grad)]
    for at in range(parts):
        place = pl.ds(at * rows, rows)
        steps.append((waves.at[:, place, :], waves_here.at[:, place, :], pres.at[:, place, :]))
    taken = [pltpu.make_async_copy(source, here, sem.at[0, at]) for at, (source, here, _) in enumerate(steps)]
    given = [pltpu.make_async_copy(here, target, sem.at[1, at]) for at, (_, here, target) in enumerate(steps)]
    for copy in taken:
        copy.start()
    for into, out in zip(taken, given):
        into.wait()
        out.start()
    for copy in given:
        copy.wait()


def shards(n_emit, n_vx, fwd_state, adj_state, courant, decay_rate, strength, footprint, owner_map):
    rows = fwd_state.shape[2]
    blocks = owner_map.shape[-1]
    per = blocks // n_emit
    padded = rows + 2 * TOP
    anywhere = pl.BlockSpec(memory_space=pl.ANY)
    far = pl.BlockSpec(memory_space=pltpu.HBM)

    def blocks_of(count):
        return pltpu.VMEM((count, per, BR, BC), jnp.float32)

    found, waves = pl.pallas_call(
        functools.partial(kernel, n_emit, n_vx, rows),
        out_shape=(jax.ShapeDtypeStruct((per, BR, BC), jnp.float32),
                   jax.ShapeDtypeStruct((1, rows, 2 * BC), jnp.float32)),
        in_specs=[far] * 7,
        out_specs=(pl.BlockSpec(memory_space=pltpu.VMEM), anywhere),
        scratch_shapes=[pltpu.VMEM((3, padded, BC), jnp.float32)] * ARRAYS + [
            pltpu.VMEM((4, 2, padded, BC), jnp.float32),
            pltpu.VMEM((2, 2, 40, BC), jnp.float32),
            pltpu.VMEM((2, 2, 40, BC), jnp.float32),
            pltpu.VMEM((rows, BC), jnp.float32),
            pltpu.VMEM((rows + 2 * HALO, BC), jnp.float32),
        ] + [blocks_of(n_emit)] * 2 + [
            pltpu.SMEM(footprint.shape, jnp.int32),
            pltpu.SMEM(owner_map.shape, jnp.int32),
            pltpu.SemaphoreType.DMA((2 * ARRAYS,)),
            pltpu.SemaphoreType.DMA((5,)),
            pltpu.SemaphoreType.DMA((5,)),
            pltpu.SemaphoreType.DMA((n_emit,)),
            pltpu.SemaphoreType.DMA((n_emit,)),
            pltpu.SemaphoreType.DMA((2,)),
            pltpu.SemaphoreType.DMA((2,)),
        ],
        compiler_params=pltpu.CompilerParams(collective_id=0, has_side_effects=True),
        name="waves",
    )(fwd_state, adj_state, courant, decay_rate, strength, footprint, owner_map)
    return pl.pallas_call(
        hand_over,
        out_shape=(jax.ShapeDtypeStruct(found.shape, jnp.float32),
                   jax.ShapeDtypeStruct(waves.shape, jnp.float32)),
        in_specs=[anywhere] * 2,
        out_specs=(anywhere, anywhere),
        scratch_shapes=[pltpu.VMEM(found.shape, jnp.float32), pltpu.VMEM(waves.shape, jnp.float32),
                        pltpu.SemaphoreType.DMA((2, 5))],
        name="hand_over",
    )(found, waves)


def solution(mesh):
    in_specs = (
        P(None, "emit", "vx", "vy"),
        P(None, "emit", "vx", "vy"),
        P("vx", "vy"),
        P("vx", "vy"),
        P("vx", "vy"),
        P("emit", "vx", "vy", None),
        P("vx", "vy", None),
    )
    out_specs = (P("emit", "vx", "vy"), P("emit", "vx", "vy"))
    body = functools.partial(shards, mesh.shape["emit"], mesh.shape["vx"])
    return jax.shard_map(body, mesh=mesh, in_specs=in_specs, out_specs=out_specs, check_vma=False)
```
